32 devices in a mesh: row: 4 (over z), col: 8 (over y, x, core).
Axes of the slice: x: 2, y: 2, z: 4, core: 2. Of those that a mesh axis runs over, the one named last changes fastest.
Arguments:
- trailing: bfloat16 [4096, 4096], P('row', 'col'), may hold values from -12 to 12
- panel_left: bfloat16 [4096, 1024], P(('row', 'col')), may hold values from -1.5 to 1.5
- panel_right: bfloat16 [4096, 1024], P(('col', 'row')), may hold values from -1.5 to 1.5
- inverse_factors: float32 [2, 512, 512], replicated, may hold values from -2 to 2, as said below
- active: int32 [8, 8], P('row', 'col'), may hold values 0 or 1
Outputs:
- updated: bfloat16 [4096, 4096], P('row', 'col')
The draws below stay inside these ranges and needn't reach their ends.
Inputs may be any that keep to these rules, and one draw needn't show every extreme that they name: `inverse_factors`: lower triangular, positive diagonal.
All inputs are finite; a program needn't handle non-finite values. No bound on the sum of `active` on one device may be relied on, other than what follows from the above.
Results may differ from the reference program's by a relative error of at most 0.0052.
Values may be sent and summed in bfloat16 or wider, within the bound.
A program may use at most 64 MiB of HBM per device.

```python
import jax
import jax.numpy as jnp
from jax import lax

TILE = 512
PANELS = 2
MT = 8
NT = 8
ROWS = 4096
COLS = 4096


def draw_inverse_factors(key, part):
    first, second = jax.random.split(jax.random.fold_in(key, 71))
    diag_vals = jnp.exp(jax.random.uniform(first, (PANELS, TILE), jnp.float32, jnp.log(0.5), jnp.log(2.0)))
    lower = jax.random.normal(second, (PANELS, TILE, TILE), jnp.float32) * (0.5 / TILE ** 0.5)
    strict = jnp.tril(lower, -1)
    eye_mat = jnp.eye(TILE, dtype=jnp.float32)
    return strict + eye_mat[None, :, :] * diag_vals[:, None, :]


def with_ends(drawn, stream_key, least, high):
    place = [jax.random.randint(jax.random.fold_in(stream_key, axis), (), 0, length) for axis, length in enumerate(drawn.shape)]
    main_axis = drawn.shape.index(max(drawn.shape))
    beside = place[:main_axis] + [(place[main_axis] + 1) % drawn.shape[main_axis]] + place[main_axis + 1:]
    return drawn.at[tuple(place)].set(least).at[tuple(beside)].set(high)


def level_of(own_key, extent, cuts, smallest, largest):
    gain = 1.0
    for axis_at, blocks in cuts:
        heights = jax.random.uniform(jax.random.fold_in(jax.random.fold_in(own_key, 6), axis_at), (blocks,), jnp.float32, smallest / len(cuts), largest / len(cuts))
        gain = gain * jnp.repeat(jnp.exp(heights), extent[axis_at] // blocks).reshape((-1,) + (1,) * (len(extent) - 1 - axis_at))
    return gain


def centred(stream_key, extent, scale, reach, cuts=(), kind=jnp.bfloat16):
    drawn = jax.random.normal(stream_key, extent, jnp.float32) * scale
    if len(cuts) > 0:
        drawn = level_of(stream_key, extent, cuts, -0.22, 0.18) * drawn
    return jnp.clip(drawn, min=-reach, max=reach).astype(kind)


def setup_inputs(seed: int = 0) -> dict:
    splits = jax.random.split(jax.random.key(seed), 6)
    return {
        "trailing": centred(splits[0], (ROWS, COLS), 2.0, 12.0, ((0, 4), (1, 8))),
        "panel_left": centred(splits[1], (ROWS, PANELS * TILE), 0.25, 1.5, ((0, 32),)),
        "panel_right": centred(splits[2], (COLS, PANELS * TILE), 0.25, 1.5, ((0, 32),)),
        "inverse_factors": draw_inverse_factors(jax.random.fold_in(splits[5], 71), 0),
        "active": with_ends((jax.random.randint(splits[4], (MT, NT), 0, 5) < 3).astype(jnp.int32), jax.random.fold_in(splits[4], 1), 0, 1),
    }


def triangle(rows, inverse_factors):
    width = inverse_factors.shape[1]
    parts = []
    for panel in range(inverse_factors.shape[0]):
        block = rows[:, panel * width:(panel + 1) * width].astype(jnp.float32)
        parts.append(jnp.dot(block, inverse_factors[panel].T, precision=lax.Precision.HIGHEST, preferred_element_type=jnp.float32))
    return jnp.concatenate(parts, axis=1).astype(jnp.bfloat16)


def reference(trailing, panel_left, panel_right, inverse_factors, active):
    factor_left = triangle(panel_left, inverse_factors)
    factor_right = triangle(panel_right, inverse_factors)
    width = inverse_factors.shape[1]
    right_tiles = factor_right.reshape(NT, width, factor_right.shape[1])
    trail_tiles = jnp.transpose(trailing.reshape(ROWS, NT, width), (1, 0, 2))
    mask_cols = jnp.transpose(active, (1, 0))

    def one_column(items):
        right_tile, trail_tile, mask_col = items
        change = lax.dot_general(factor_left, right_tile, (((1,), (1,)), ((), ())), preferred_element_type=jnp.float32)
        keep = jnp.repeat(mask_col, width)[:, None] == 1
        fresh = trail_tile.astype(jnp.float32) - change
        return jnp.where(keep, fresh, trail_tile.astype(jnp.float32)).astype(jnp.bfloat16)

    columns = lax.map(one_column, (right_tiles, trail_tiles, mask_cols))
    return jnp.transpose(columns, (1, 0, 2)).reshape(ROWS, COLS)
```

```python
import functools

import jax
import jax.numpy as jnp
from jax import lax
from jax.experimental import pallas as pl
from jax.experimental.pallas import tpu as pltpu
from jax.sharding import PartitionSpec as P

MESH = pl.DeviceIdType.MESH
NT_DIMS = (((1,), (1,)), ((), ()))


def dot_nt(a, b):
    return lax.dot_general(a, b, NT_DIMS, preferred_element_type=jnp.float32)


def triangle(rows, inverse_factors):
    width = inverse_factors.shape[1]
    parts = []
    for panel in range(inverse_factors.shape[0]):
        block = rows[:, panel * width : (panel + 1) * width].astype(jnp.float32)
        parts.append(
            jnp.dot(
                block,
                inverse_factors[panel].T,
                precision=lax.Precision.HIGHEST,
                preferred_element_type=jnp.float32,
            )
        )
    return jnp.concatenate(parts, axis=1).astype(jnp.bfloat16)


def local_plain(trailing, panel_left, panel_right, inverse_factors, active):
    width = inverse_factors.shape[1]
    factor_left = triangle(panel_left, inverse_factors)
    factor_right = triangle(panel_right, inverse_factors)
    change = jnp.zeros(trailing.shape, jnp.float32)
    for panel in range(inverse_factors.shape[0]):
        cols = slice(panel * width, (panel + 1) * width)
        right_part = lax.all_gather(factor_right[:, cols], "row", axis=0, tiled=True)
        left_part = lax.all_gather(factor_left[:, cols], "col", axis=0, tiled=True)
        change = change + dot_nt(left_part, right_part)
    tile_rows, tile_cols = active.shape
    shaped = trailing.astype(jnp.float32).reshape(tile_rows, width, tile_cols, width)
    fresh = shaped - change.reshape(tile_rows, width, tile_cols, width)
    keep = active[:, None, :, None] == 1
    result = jnp.where(keep, fresh, shaped).astype(jnp.bfloat16)
    return result.reshape(trailing.shape)


def flip(chip, mask):
    bit = 1
    while bit <= mask:
        if mask & bit:
            chip = chip + (1 - 2 * ((chip // bit) % 2)) * bit
        bit *= 2
    return chip


def kernel(
    nr, nc, tile_cols,
    tr_hbm, left_hbm, right_hbm, inv_hbm, act_ref, out_ref,
    trv, lv, rv, invv, ih, il, rbuf, lbuf, fbuf, acc, outv,
    in_sem, inv_sem, tr_sem, out_sem, rsend, rrecv, lsend, lrecv, fsend,
):
    panels, width = ih.shape[0], ih.shape[1]
    half = width // 2
    chunks = 2 * panels
    ml, mr = lv.shape[0], rv.shape[0]
    rows = trv.shape[1]
    chips = nc // 2
    z = lax.axis_index("row")
    c = lax.axis_index("col")
    chip, core = c // 2, c % 2
    sib = chip * 2 + 1 - core

    def peer(j):
        return flip(chip, j) * 2 + core

    def other(j):
        return flip(chip, j) * 2 + 1 - core

    def cols(piece):
        return pl.ds(pl.multiple_of(piece * mr, mr), mr)

    barrier = pltpu.get_barrier_semaphore()

    def greet(dev):
        pl.semaphore_signal(barrier, inc=1, device_id=dev, device_id_type=MESH)

    @pl.when(z > 0)
    def _():
        greet((z - 1, c))

    @pl.when(z < nr - 1)
    def _():
        greet((z + 1, c))

    greet((z, sib))
    for j in range(1, chips):
        greet((z, peer(j)))

    load_left = pltpu.make_async_copy(left_hbm, lv, in_sem.at[0])
    load_right = pltpu.make_async_copy(right_hbm, rv, in_sem.at[1])
    load_inv = [
        pltpu.make_async_copy(inv_hbm.at[p], invv.at[p], inv_sem.at[p])
        for p in range(panels)
    ]
    load_left.start()
    load_right.start()
    for cp in load_inv:
        cp.start()
    load_tr = [
        pltpu.make_async_copy(
            tr_hbm.at[:, i * mr : (i + 1) * mr], trv.at[i], tr_sem.at[i]
        )
        for i in range(nr)
    ]
    for cp in load_tr:
        cp.start()

    ends = jnp.where(z > 0, 1, 0) + jnp.where(z < nr - 1, 1, 0)
    pl.semaphore_wait(barrier, ends + chips)

    def right_copy(d, t, q):
        to = z - 1 if d == 0 else z + 1
        origin = z + t if d == 0 else z - t
        src = (
            right_hbm.at[:, q * half : (q + 1) * half]
            if t == 0
            else rbuf.at[origin, q]
        )
        return pltpu.make_async_remote_copy(
            src_ref=src,
            dst_ref=rbuf.at[origin, q],
            send_sem=rsend.at[d, t, q],
            recv_sem=rrecv.at[d, t, q],
            device_id=(to, c),
            device_id_type=MESH,
        )

    def right_sends(d, t):
        if d == 0:
            return jnp.logical_and(z > 0, z + t < nr)
        return jnp.logical_and(z < nr - 1, z - t >= 0)

    def right_has(d, s):
        return z + s < nr if d == 0 else z - s >= 0

    for d in range(2):
        @pl.when(right_sends(d, 0))
        def _():
            for q in range(chunks):
                right_copy(d, 0, q).start()

    def left_copy(p, dev, origin, sems, j):
        return pltpu.make_async_remote_copy(
            src_ref=lbuf.at[p, origin],
            dst_ref=lbuf.at[p, origin],
            send_sem=sems.at[p, j],
            recv_sem=lrecv.at[p, origin],
            device_id=(z, dev),
            device_id_type=MESH,
        )

    def factor(part0, part1, p):
        first = dot_nt(part0, ih[p, :half, :half]) + dot_nt(part0, il[p, :half, :half])
        second = (
            dot_nt(part0, ih[p, half:, :half])
            + dot_nt(part1, ih[p, half:, half:])
            + dot_nt(part0, il[p, half:, :half])
            + dot_nt(part1, il[p, half:, half:])
        )
        return first.astype(jnp.bfloat16), second.astype(jnp.bfloat16)

    load_left.wait()
    for p in range(panels):
        load_inv[p].wait()
        whole = invv[p]
        high = whole.astype(jnp.bfloat16)
        ih[p] = high
        il[p] = (whole - high.astype(jnp.float32)).astype(jnp.bfloat16)
        a = lv[:, p * width : p * width + half]
        b = lv[:, p * width + half : (p + 1) * width]
        first, second = factor(a, b, p)
        lbuf[p, c, :, :half] = first
        lbuf[p, c, :, half:] = second
        for j in range(1, chips):
            left_copy(p, peer(j), c, lsend, j).start()
        left_copy(p, sib, c, lsend, 0).start()

    load_right.wait()
    for p in range(panels):
        a = rv[:, p * width : p * width + half]
        b = rv[:, p * width + half : (p + 1) * width]
        first, second = factor(a, b, p)
        fbuf[p, z, :, :half] = first
        fbuf[p, z, :, half:] = second

    def right_arrive(s, p):
        for d in range(2):
            origin = z + s if d == 0 else z - s

            @pl.when(right_has(d, s))
            def _():
                for h in range(2):
                    q = 2 * p + h
                    right_copy(d, s - 1, q).wait_recv()
                    if s < nr - 1:
                        @pl.when(right_sends(d, s))
                        def _():
                            right_copy(d, s, q).start()
                first, second = factor(rbuf[origin, 2 * p], rbuf[origin, 2 * p + 1], p)
                fbuf[p, origin, :, :half] = first
                fbuf[p, origin, :, half:] = second

    def left_arrive(p):
        for j in range(1, chips):
            left_copy(p, peer(j), peer(j), lsend, j).wait_recv()
            left_copy(p, sib, peer(j), fsend, j).start()

    def left_rest(p):
        for j in range(chips):
            left_copy(p, sib, other(j), lsend, 0).wait_recv()

    def product(p, piece):
        left = lbuf[p].reshape(nc * ml, width)
        return dot_nt(left, fbuf[p, piece])

    def begin(p, piece):
        if p == 0:
            acc[piece] = product(p, piece)
        else:
            acc[piece] += product(p, piece)

    def finish(piece):
        change = product(panels - 1, piece)
        if panels > 1:
            change = acc[piece] + change
        tc = (piece * mr) // width
        for t in range(rows // width):
            span = slice(t * width, (t + 1) * width)
            old = trv[piece, span].astype(jnp.float32)
            keep = jnp.full(old.shape, act_ref[t * tile_cols + tc], jnp.int32) == 1
            new = jnp.where(keep, old - change[span], old)
            outv[piece, span] = new.astype(jnp.bfloat16)
        pltpu.make_async_copy(
            outv.at[piece], out_ref.at[:, cols(piece)], out_sem.at[piece]
        ).start()

    def at_step(s, fn):
        if s == 0:
            fn(z)
            return
        for d in range(2):
            @pl.when(right_has(d, s))
            def _():
                fn(z + s if d == 0 else z - s)

    last = nr - 1
    for s in range(1, last):
        for p in range(panels):
            right_arrive(s, p)
        if s == 1:
            for p in range(panels - 1):
                left_arrive(p)
    if last < 2:
        for p in range(panels - 1):
            left_arrive(p)
    for p in range(panels - 1):
        left_rest(p)
        for s in range(last):
            at_step(s, functools.partial(begin, p))
    left_arrive(panels - 1)
    for cp in load_tr:
        cp.wait()
    for p in range(panels - 1):
        if last > 0:
            right_arrive(last, p)
            at_step(last, functools.partial(begin, p))
    left_rest(panels - 1)
    for s in range(last):
        at_step(s, finish)
    if last > 0:
        right_arrive(last, panels - 1)
        at_step(last, finish)

    for d in range(2):
        for t in range(nr - 1):
            @pl.when(right_sends(d, t))
            def _():
                for q in range(chunks):
                    right_copy(d, t, q).wait_send()
    for p in range(panels):
        for j in range(1, chips):
            left_copy(p, peer(j), c, lsend, j).wait_send()
            left_copy(p, sib, peer(j), fsend, j).wait_send()
        left_copy(p, sib, c, lsend, 0).wait_send()
    for piece in range(nr):
        pltpu.make_async_copy(
            outv.at[piece], out_ref.at[:, piece * mr : (piece + 1) * mr], out_sem.at[piece]
        ).wait()


def local(nr, nc, trailing, panel_left, panel_right, inverse_factors, active):
    panels, width = inverse_factors.shape[:2]
    half = width // 2
    rows, _ = trailing.shape
    ml, depth = panel_left.shape
    mr = panel_right.shape[0]
    chips = nc // 2
    if ml % 16 or mr % 128 or half % 128 or width % mr or nc % 2 or chips & (chips - 1) or nr < 2:
        return local_plain(trailing, panel_left, panel_right, inverse_factors, active)
    bf16, f32 = jnp.bfloat16, jnp.float32
    anywhere = pl.BlockSpec(memory_space=pl.ANY)
    return pl.pallas_call(
        functools.partial(kernel, nr, nc, active.shape[1]),
        out_shape=jax.ShapeDtypeStruct(trailing.shape, bf16),
        in_specs=[anywhere] * 4 + [pl.BlockSpec(memory_space=pltpu.SMEM)],
        out_specs=anywhere,
        scratch_shapes=[
            pltpu.VMEM((nr, rows, mr), bf16),
            pltpu.VMEM((ml, depth), bf16),
            pltpu.VMEM((mr, depth), bf16),
            pltpu.VMEM((panels, width, width), f32),
            pltpu.VMEM((panels, width, width), bf16),
            pltpu.VMEM((panels, width, width), bf16),
            pltpu.VMEM((nr, 2 * panels, mr, half), bf16),
            pltpu.VMEM((panels, nc, ml, width), bf16),
            pltpu.VMEM((panels, nr, mr, width), bf16),
            pltpu.VMEM((nr, rows, mr), f32),
            pltpu.VMEM((nr, rows, mr), bf16),
            pltpu.SemaphoreType.DMA((2,)),
            pltpu.SemaphoreType.DMA((panels,)),
            pltpu.SemaphoreType.DMA((nr,)),
            pltpu.SemaphoreType.DMA((nr,)),
            pltpu.SemaphoreType.DMA((2, nr - 1, 2 * panels)),
            pltpu.SemaphoreType.DMA((2, nr - 1, 2 * panels)),
            pltpu.SemaphoreType.DMA((panels, chips)),
            pltpu.SemaphoreType.DMA((panels, nc)),
            pltpu.SemaphoreType.DMA((panels, chips)),
        ],
        compiler_params=pltpu.CompilerParams(
            collective_id=0, has_side_effects=True, vmem_limit_bytes=40 * 2**20
        ),
        name="trailing_update",
    )(trailing, panel_left, panel_right, inverse_factors, active.reshape(-1))


def solution(mesh):
    in_specs = (
        P("row", "col"),
        P(("row", "col"), None),
        P(("col", "row"), None),
        P(),
        P("row", "col"),
    )
    body = functools.partial(local, mesh.shape["row"], mesh.shape["col"])
    return jax.shard_map(
        body, mesh=mesh, in_specs=in_specs, out_specs=P("row", "col"), check_vma=False
    )
```

```python
import functools

import jax
import jax.numpy as jnp
from jax import lax
from jax.experimental import pallas as pl
from jax.experimental.pallas import tpu as pltpu
from jax.sharding import PartitionSpec as P

MESH = pl.DeviceIdType.MESH
NT_DIMS = (((1,), (1,)), ((), ()))


def dot_nt(a, b):
    return lax.dot_general(a, b, NT_DIMS, preferred_element_type=jnp.float32)


def triangle(rows, inverse_factors):
    width = inverse_factors.shape[1]
    parts = []
    for panel in range(inverse_factors.shape[0]):
        block = rows[:, panel * width : (panel + 1) * width].astype(jnp.float32)
        parts.append(
            jnp.dot(
                block,
                inverse_factors[panel].T,
                precision=lax.Precision.HIGHEST,
                preferred_element_type=jnp.float32,
            )
        )
    return jnp.concatenate(parts, axis=1).astype(jnp.bfloat16)


def local_plain(trailing, panel_left, panel_right, inverse_factors, active):
    width = inverse_factors.shape[1]
    factor_left = triangle(panel_left, inverse_factors)
    factor_right = triangle(panel_right, inverse_factors)
    change = jnp.zeros(trailing.shape, jnp.float32)
    for panel in range(inverse_factors.shape[0]):
        cols = slice(panel * width, (panel + 1) * width)
        right_part = lax.all_gather(factor_right[:, cols], "row", axis=0, tiled=True)
        left_part = lax.all_gather(factor_left[:, cols], "col", axis=0, tiled=True)
        change = change + dot_nt(left_part, right_part)
    tile_rows, tile_cols = active.shape
    shaped = trailing.astype(jnp.float32).reshape(tile_rows, width, tile_cols, width)
    fresh = shaped - change.reshape(tile_rows, width, tile_cols, width)
    keep = active[:, None, :, None] == 1
    result = jnp.where(keep, fresh, shaped).astype(jnp.bfloat16)
    return result.reshape(trailing.shape)


def flip(chip, mask):
    bit = 1
    while bit <= mask:
        if mask & bit:
            chip = chip + (1 - 2 * ((chip // bit) % 2)) * bit
        bit *= 2
    return chip


def kernel(
    nr, nc, tile_cols,
    tr_hbm, left_hbm, right_hbm, inv_hbm, act_ref, out_ref,
    trv, lv, rv, invv, ih, il, rbuf, lbuf, fbuf, acc, outv,
    in_sem, inv_sem, tr_sem, out_sem, rsend, rrecv, lsend, lrecv, fsend,
):
    panels, width = ih.shape[0], ih.shape[1]
    half = width // 2
    chunks = 2 * panels
    ml, mr = lv.shape[0], rv.shape[0]
    rows = trv.shape[1]
    chips = nc // 2
    z = lax.axis_index("row")
    c = lax.axis_index("col")
    chip, core = c // 2, c % 2
    sib = chip * 2 + 1 - core

    def peer(j):
        return flip(chip, j) * 2 + core

    def other(j):
        return flip(chip, j) * 2 + 1 - core

    def cols(piece):
        return pl.ds(pl.multiple_of(piece * mr, mr), mr)

    barrier = pltpu.get_barrier_semaphore()

    def greet(dev):
        pl.semaphore_signal(barrier, inc=1, device_id=dev, device_id_type=MESH)

    @pl.when(z > 0)
    def _():
        greet((z - 1, c))

    @pl.when(z < nr - 1)
    def _():
        greet((z + 1, c))

    greet((z, sib))
    for j in range(1, chips):
        greet((z, peer(j)))

    load_left = pltpu.make_async_copy(left_hbm, lv, in_sem.at[0])
    load_right = pltpu.make_async_copy(right_hbm, rv, in_sem.at[1])
    load_inv = [
        pltpu.make_async_copy(inv_hbm.at[p], invv.at[p], inv_sem.at[p])
        for p in range(panels)
    ]
    load_right.start()
    for cp in load_inv[1:]:
        cp.start()
    load_left.start()
    load_inv[0].start()
    load_tr = [
        pltpu.make_async_copy(
            tr_hbm.at[:, i * mr : (i + 1) * mr], trv.at[i], tr_sem.at[i]
        )
        for i in range(nr)
    ]
    for cp in load_tr:
        cp.start()

    ends = jnp.where(z > 0, 1, 0) + jnp.where(z < nr - 1, 1, 0)
    pl.semaphore_wait(barrier, ends + chips)

    def right_copy(d, t, q):
        to = z - 1 if d == 0 else z + 1
        origin = z + t if d == 0 else z - t
        slot = rbuf.at[origin, q] if q < 2 else fbuf.at[q, origin]
        own = q < 2 and t == 0
        return pltpu.make_async_remote_copy(
            src_ref=right_hbm.at[:, q * half : (q + 1) * half] if own else slot,
            dst_ref=slot,
            send_sem=rsend.at[d, t, q],
            recv_sem=rrecv.at[d, t, q],
            device_id=(to, c),
            device_id_type=MESH,
        )

    def right_sends(d, t):
        if d == 0:
            return jnp.logical_and(z > 0, z + t < nr)
        return jnp.logical_and(z < nr - 1, z - t >= 0)

    def right_has(d, s):
        return z + s < nr if d == 0 else z - s >= 0

    def right_own(qs):
        for d in range(2):
            @pl.when(right_sends(d, 0))
            def _():
                for q in qs:
                    right_copy(d, 0, q).start()

    right_own(range(2))

    def left_copy(p, dev, origin, sems, j):
        return pltpu.make_async_remote_copy(
            src_ref=lbuf.at[p, origin],
            dst_ref=lbuf.at[p, origin],
            send_sem=sems.at[p, j],
            recv_sem=lrecv.at[p, origin],
            device_id=(z, dev),
            device_id_type=MESH,
        )

    def factor(part0, part1, p):
        first = dot_nt(part0, ih[p, :half, :half]) + dot_nt(part0, il[p, :half, :half])
        second = (
            dot_nt(part0, ih[p, half:, :half])
            + dot_nt(part1, ih[p, half:, half:])
            + dot_nt(part0, il[p, half:, :half])
            + dot_nt(part1, il[p, half:, half:])
        )
        return first.astype(jnp.bfloat16), second.astype(jnp.bfloat16)

    def halves(ref, p):
        return (
            ref[:, p * width : p * width + half],
            ref[:, p * width + half : (p + 1) * width],
        )

    def factor_right(a, b, p, piece):
        fbuf[2 * p, piece], fbuf[2 * p + 1, piece] = factor(a, b, p)

    def split(p):
        load_inv[p].wait()
        whole = invv[p]
        high = whole.astype(jnp.bfloat16)
        ih[p] = high
        il[p] = (whole - high.astype(jnp.float32)).astype(jnp.bfloat16)

    load_right.wait()
    for p in range(1, panels):
        split(p)
        factor_right(*halves(rv, p), p, z)
        right_own((2 * p, 2 * p + 1))

    load_left.wait()
    for p in range(panels):
        if p == 0:
            split(p)
        first, second = factor(*halves(lv, p), p)
        lbuf[p, c, :, :half] = first
        lbuf[p, c, :, half:] = second
        for j in range(1, chips):
            left_copy(p, peer(j), c, lsend, j).start()
        left_copy(p, sib, c, lsend, 0).start()
    factor_right(*halves(rv, 0), 0, z)

    def at_step(s, fn):
        if s == 0:
            fn(0, z)
            return
        for d in range(2):
            @pl.when(right_has(d, s))
            def _():
                fn(d, z + s if d == 0 else z - s)

    def right_arrive(s, qs):
        def take(d, origin):
            for q in qs:
                right_copy(d, s - 1, q).wait_recv()
                if s < nr - 1:
                    @pl.when(right_sends(d, s))
                    def _():
                        right_copy(d, s, q).start()
            if 0 in qs:
                factor_right(rbuf[origin, 0], rbuf[origin, 1], 0, origin)

        at_step(s, take)

    def left_arrive(p):
        for j in range(1, chips):
            left_copy(p, peer(j), peer(j), lsend, j).wait_recv()
            left_copy(p, sib, peer(j), fsend, j).start()

    def left_rest(p):
        for j in range(chips):
            left_copy(p, sib, other(j), lsend, 0).wait_recv()

    def product(qs, piece):
        total = None
        for q in qs:
            lo = (q % 2) * half
            left = lbuf[q // 2, :, :, lo : lo + half].reshape(nc * ml, half)
            part = dot_nt(left, fbuf[q, piece])
            total = part if total is None else total + part
        return total

    def store(piece):
        return pltpu.make_async_copy(
            outv.at[piece], out_ref.at[:, cols(piece)], out_sem.at[piece]
        )

    def begin(qs, d, piece):
        if 0 in qs:
            acc[piece] = product(qs, piece)
        else:
            acc[piece] += product(qs, piece)

    def finish(qs, d, piece):
        change = product(qs, piece)
        if 0 not in qs:
            change = acc[piece] + change
        tc = (piece * mr) // width
        for t in range(rows // width):
            span = slice(t * width, (t + 1) * width)
            old = trv[piece, span].astype(jnp.float32)
            keep = jnp.full(old.shape, act_ref[t * tile_cols + tc], jnp.int32) == 1
            new = jnp.where(keep, old - change[span], old)
            outv[piece, span] = new.astype(jnp.bfloat16)
        store(piece).start()

    def panel(p):
        return (2 * p, 2 * p + 1)

    def add(fn, s, qs):
        at_step(s, functools.partial(fn, qs))

    last = nr - 1
    for s in range(1, last):
        right_arrive(s, range(chunks))
        if s == 1:
            for p in range(panels - 1):
                left_arrive(p)
    if last < 2:
        for p in range(panels - 1):
            left_arrive(p)
    for p in range(panels - 1):
        left_rest(p)
        for s in range(last):
            add(begin, s, panel(p))
    left_arrive(panels - 1)
    for cp in load_tr:
        cp.wait()
    for p in range(panels - 1):
        right_arrive(last, panel(p))
        add(begin, last, panel(p))
    left_rest(panels - 1)
    for s in range(last):
        add(finish, s, panel(panels - 1))
    if panels > 1:
        right_arrive(last, (chunks - 2,))
        add(begin, last, (chunks - 2,))
        right_arrive(last, (chunks - 1,))
        add(finish, last, (chunks - 1,))
    else:
        right_arrive(last, panel(0))
        add(finish, last, panel(0))

    for d in range(2):
        for t in range(nr - 1):
            @pl.when(right_sends(d, t))
            def _():
                for q in range(chunks):
                    right_copy(d, t, q).wait_send()
    for p in range(panels):
        for j in range(1, chips):
            left_copy(p, peer(j), c, lsend, j).wait_send()
            left_copy(p, sib, peer(j), fsend, j).wait_send()
        left_copy(p, sib, c, lsend, 0).wait_send()
    for s in range(nr):
        at_step(s, lambda d, piece: store(piece).wait())


def local(nr, nc, trailing, panel_left, panel_right, inverse_factors, active):
    panels, width = inverse_factors.shape[:2]
    half = width // 2
    rows, _ = trailing.shape
    ml, depth = panel_left.shape
    mr = panel_right.shape[0]
    chips = nc // 2
    if ml % 16 or mr % 128 or half % 128 or width % mr or nc % 2 or chips & (chips - 1) or nr < 2:
        return local_plain(trailing, panel_left, panel_right, inverse_factors, active)
    bf16, f32 = jnp.bfloat16, jnp.float32
    anywhere = pl.BlockSpec(memory_space=pl.ANY)
    return pl.pallas_call(
        functools.partial(kernel, nr, nc, active.shape[1]),
        out_shape=jax.ShapeDtypeStruct(trailing.shape, bf16),
        in_specs=[anywhere] * 4 + [pl.BlockSpec(memory_space=pltpu.SMEM)],
        out_specs=anywhere,
        scratch_shapes=[
            pltpu.VMEM((nr, rows, mr), bf16),
            pltpu.VMEM((ml, depth), bf16),
            pltpu.VMEM((mr, depth), bf16),
            pltpu.VMEM((panels, width, width), f32),
            pltpu.VMEM((panels, width, width), bf16),
            pltpu.VMEM((panels, width, width), bf16),
            pltpu.VMEM((nr, 2, mr, half), bf16),
            pltpu.VMEM((panels, nc, ml, width), bf16),
            pltpu.VMEM((2 * panels, nr, mr, half), bf16),
            pltpu.VMEM((nr, rows, mr), f32),
            pltpu.VMEM((nr, rows, mr), bf16),
            pltpu.SemaphoreType.DMA((2,)),
            pltpu.SemaphoreType.DMA((panels,)),
            pltpu.SemaphoreType.DMA((nr,)),
            pltpu.SemaphoreType.DMA((nr,)),
            pltpu.SemaphoreType.DMA((2, nr - 1, 2 * panels)),
            pltpu.SemaphoreType.DMA((2, nr - 1, 2 * panels)),
            pltpu.SemaphoreType.DMA((panels, chips)),
            pltpu.SemaphoreType.DMA((panels, nc)),
            pltpu.SemaphoreType.DMA((panels, chips)),
        ],
        compiler_params=pltpu.CompilerParams(
            collective_id=0, has_side_effects=True, vmem_limit_bytes=58 * 2**20
        ),
        name="trailing_update",
    )(trailing, panel_left, panel_right, inverse_factors, active.reshape(-1))


def solution(mesh):
    in_specs = (
        P("row", "col"),
        P(("row", "col"), None),
        P(("col", "row"), None),
        P(),
        P("row", "col"),
    )
    body = functools.partial(local, mesh.shape["row"], mesh.shape["col"])
    return jax.shard_map(
        body, mesh=mesh, in_specs=in_specs, out_specs=P("row", "col"), check_vma=False
    )
```
